32 devices in a mesh: grp: 2 (over x), ctx: 8 (over z, y), exp: 2 (over core).
Axes of the slice: x: 2, y: 2, z: 4, core: 2. Of those that a mesh axis runs over, the one named last changes fastest.
Arguments:
- queries: bfloat16 [128, 3072], P(('grp', 'ctx'), 'exp'), parts along dimension 0, may hold values from -8 to 8
- fresh_keys: bfloat16 [128, 512], P(('grp', 'ctx'), 'exp'), parts along dimension 0, may hold values from -4 to 4
- fresh_values: bfloat16 [128, 512], P(('grp', 'ctx'), 'exp'), parts along dimension 0, may hold values from -5 to 5
- prefix_key_cache: bfloat16 [8192, 512], P(('grp', 'ctx'), 'exp'), parts along dimension 0, may hold values from -4 to 4
- prefix_value_cache: bfloat16 [8192, 512], P(('grp', 'ctx'), 'exp'), parts along dimension 0, may hold values from -5 to 5
- prefix_len: int32 [2], P('grp'), parts along dimension 0, may hold values from 2048 to 4096
- residual: bfloat16 [128, 6144], P(('grp', 'ctx')), parts along dimension 0, may hold values from -6 to 6
- out_proj: bfloat16 [3072, 6144], P('exp', 'ctx'), may hold values from -0.21875 to 0.21875
- norm_gain: float32 [6144], replicated, may hold values from 0.25 to 1.75
- routes: int32 [128, 2], P(('grp', 'ctx')), parts along dimension 0, may hold values from 0 to 7, all different within a row; in each aligned block of 8 rows (0 to 7, 8 to 15, ...) at most 3 rows name the same one
- route_weight: float32 [128, 2], P(('grp', 'ctx')), parts along dimension 0, may hold values from 0.1 to 1
- w_gate: bfloat16 [2, 6144, 16384], P('exp', None, 'ctx'), may hold values from -0.078125 to 0.078125
- w_up: bfloat16 [2, 6144, 16384], P('exp', None, 'ctx'), may hold values from -0.078125 to 0.078125
- w_down: bfloat16 [2, 16384, 6144], P('exp', 'ctx'), may hold values from -0.09375 to 0.09375
Outputs:
- layer_out: bfloat16 [128, 6144], P(('grp', 'ctx')), parts along dimension 0
The draws below stay inside these ranges and needn't reach their ends.
There are 2 independent parts, one for each index of `grp`. The reference program is written for one: setup_inputs(seed, part) draws one part's arguments, and reference() takes and returns one part's arrays. A program takes and returns all parts, laid end to end along the dimension named above; an argument that names none is the same for every part. Nothing has to cross between parts.
Inputs may be any that keep to these rules, and one draw needn't show every extreme that they name: `routes`: in every aligned block of 8 rows (the tokens of one index of ctx) no expert is named by more than 3 rows.
All inputs are finite; a program needn't handle non-finite values.
Results may differ from the reference program's by a relative error of at most 0.0059.
Values may be sent and summed in bfloat16 or wider, within the bound.
A program may use at most 192 MiB of HBM per device.

```python
import math
import jax
import jax.numpy as jnp
import numpy as np
from jax import lax

D = 6144
QUERY_HEADS = 24
KEY_VALUE_HEADS = 4
HEAD_WIDTH = 128
EXPERTS = 8
TOP = 2
FF = 16384
TOK_DEV = 8
PROMPT_TOKENS = 64
PREFIX_SLOT_COUNT = 4096
SLOTS = 3
FLIGHT = 2


def draw_queries(key, part):
    key = jax.random.fold_in(key, 1)
    output_sample = jnp.clip(3.0 * jax.random.normal(key, (PROMPT_TOKENS, QUERY_HEADS, HEAD_WIDTH), jnp.float32), -8.0, 8.0)
    return output_sample.reshape(PROMPT_TOKENS, QUERY_HEADS * HEAD_WIDTH).astype(jnp.bfloat16)


def draw_prefix_key_cache(key, part):
    key = jax.random.fold_in(key, 2)
    output_sample = jnp.clip(jax.random.normal(key, (PREFIX_SLOT_COUNT, KEY_VALUE_HEADS, HEAD_WIDTH), jnp.float32), -4.0, 4.0)
    return output_sample.reshape(PREFIX_SLOT_COUNT, KEY_VALUE_HEADS * HEAD_WIDTH).astype(jnp.bfloat16)


def block_levels(stream_key, dims, shards, low, largest):
    factor_of = 1.0
    for dim, shards_of in shards:
        draws = jax.random.uniform(jax.random.fold_in(jax.random.fold_in(stream_key, 6), dim), (shards_of,), jnp.float32, low / len(shards), largest / len(shards))
        factor_of = factor_of * jnp.repeat(jnp.exp(draws), dims[dim] // shards_of).reshape((-1,) + (1,) * (len(dims) - 1 - dim))
    return factor_of


def routed_block(rng, own, number, rows, number_of, top, limit, skew):
    ranking = jax.random.permutation(rng, number_of)
    crowded, ordinary = load_shares(number_of, rows * top, limit, skew, True), load_shares(number_of, rows * top, limit, skew, False)
    places = jnp.arange(number_of)

    def named(lengths, turn):
        used = int((lengths > 0).sum())
        fixed = max(1, used // 4)
        passed = fixed + (places - fixed + turn * (used - fixed)) % max(1, number_of - fixed)
        return jnp.zeros((number_of,), jnp.int32).at[ranking[jnp.where(places < fixed, places, passed)]].set(jnp.asarray(lengths, jnp.int32))

    lengths = jnp.where(number % 4 == 0, named(crowded, number // 4), named(ordinary, number - number // 4 - 1))
    mixed = jax.random.permutation(jax.random.fold_in(own, 3), number_of)
    source_of, taker = mixed[0:number_of // 2 * 2:2], mixed[1:number_of // 2 * 2:2]
    room = jnp.minimum(lengths[source_of] - 1, limit - lengths[taker]) // 2
    room = jnp.where((source_of == ranking[0]) | (taker == ranking[0]) | (lengths[taker] == 0), 0, jnp.maximum(room, 0))
    passed = jax.random.randint(jax.random.fold_in(own, 4), (number_of // 2,), 0, 1 << 20) % (room + 1)
    lengths = lengths.at[source_of].add(-passed).at[taker].add(passed)
    labels = jnp.searchsorted(jnp.cumsum(lengths), jnp.arange(rows * top), side="right").astype(jnp.int32)
    grid = labels.reshape(top, rows).T
    grid = grid[jax.random.permutation(jax.random.fold_in(own, 1), rows)]
    turn = jax.random.randint(jax.random.fold_in(own, 2), (rows, 1), 0, top)
    return jnp.take_along_axis(grid, (jnp.arange(top)[None, :] + turn) % top, axis=1)


def load_shares(amount, total, reach, lean, full):
    loads = [(1 << 20) // math.isqrt(grade ** lean) + 1 for grade in range(1, amount + 1)]
    largest = reach if full else min(reach, max(-(-total // amount), total * loads[0] // sum(loads)))
    least = 1 if total - largest >= amount - 1 else 0
    holding, spare = [largest] + [least] * (amount - 1), total - largest - least * (amount - 1)
    while spare > 0:
        movable = [i for i in range(1, amount) if holding[i] < largest] or [i for i in range(1, amount) if holding[i] < reach]
        whole, remaining = sum([loads[i] for i in movable]), spare
        for i in movable:
            more = min(reach - holding[i], max(1, remaining * loads[i] // whole), spare)
            holding[i] = holding[i] + more
            spare = spare - more
    return np.array(holding)


def centred(own_key, dims, scale, most, pieces=(), held_as=jnp.bfloat16):
    array = jax.random.normal(own_key, dims, jnp.float32) * scale
    if len(pieces) > 0:
        array = block_levels(own_key, dims, pieces, -0.22, 0.18) * array
    return jnp.clip(array, min=-most, max=most).astype(held_as)


def setup_inputs(seed: int = 0, part: int = 0) -> dict:
    keys = jax.random.split(jax.random.key(seed), 15)
    own_keys = jax.random.split(jax.random.fold_in(keys[14], part), 15)
    queries = draw_queries(jax.random.fold_in(jax.random.fold_in(keys[14], part), 71), part)
    fresh_keys = centred(own_keys[1], (PROMPT_TOKENS, KEY_VALUE_HEADS * HEAD_WIDTH), 1.0, 4.0, ((0, 8), (1, 2)))
    fresh_values = centred(own_keys[2], (PROMPT_TOKENS, KEY_VALUE_HEADS * HEAD_WIDTH), 1.0, 5.0, ((0, 8), (1, 2)))
    prefix_key_cache = draw_prefix_key_cache(jax.random.fold_in(jax.random.fold_in(keys[14], part), 71), part)
    prefix_value_cache = centred(own_keys[4], (PREFIX_SLOT_COUNT, KEY_VALUE_HEADS * HEAD_WIDTH), 1.0, 5.0, ((0, 8), (1, 2)))
    prefix_len = jax.random.randint(own_keys[5], (1,), PREFIX_SLOT_COUNT // 2, PREFIX_SLOT_COUNT + 1).astype(jnp.int32)
    residual = centred(own_keys[6], (PROMPT_TOKENS, D), 1.0, 6.0, ((0, 8),))
    out_proj = centred(keys[7], (QUERY_HEADS * HEAD_WIDTH, D), (QUERY_HEADS * HEAD_WIDTH // 4) ** -0.5, 0.21875, ((0, 2), (1, 8)))
    norm_gain = jnp.clip(1.0 + 0.15 * jax.random.normal(keys[8], (D,), jnp.float32), 0.25, 1.75)
    routes_keys = jax.random.split(jax.random.fold_in(own_keys[9], 1), PROMPT_TOKENS // TOK_DEV)
    routes_turns = jax.random.permutation(jax.random.fold_in(own_keys[9], 3), PROMPT_TOKENS // TOK_DEV)
    routes = jax.vmap(lambda own, number: routed_block(jax.random.fold_in(own_keys[9], 2), own, number, TOK_DEV, EXPERTS, TOP, SLOTS, 2))(routes_keys, routes_turns).reshape((PROMPT_TOKENS, TOP))
    route_weight = jnp.clip(0.1 + 0.9 * jax.random.uniform(own_keys[10], (PROMPT_TOKENS, TOP), jnp.float32) ** block_levels(own_keys[10], (PROMPT_TOKENS, TOP), ((0, 8),), -0.2, 0.2), 0.1, 1.0)
    w_gate = centred(keys[11], (FLIGHT, D, FF), D ** -0.5, 0.078125, ((0, 2), (2, 8)))
    w_up = centred(keys[12], (FLIGHT, D, FF), D ** -0.5, 0.078125, ((0, 2), (2, 8)))
    w_down = centred(keys[13], (FLIGHT, FF, D), (FF // 4) ** -0.5, 0.09375, ((0, 2), (1, 8)))
    return dict(queries=queries, fresh_keys=fresh_keys, fresh_values=fresh_values, prefix_key_cache=prefix_key_cache, prefix_value_cache=prefix_value_cache, prefix_len=prefix_len, residual=residual, out_proj=out_proj, norm_gain=norm_gain, routes=routes, route_weight=route_weight, w_gate=w_gate, w_up=w_up, w_down=w_down)


masked_floor = -1e+30

def attend(queries, key_matrix, value_matrix, prefix):
    block_of_rows = min(64, PROMPT_TOKENS)
    head_group = QUERY_HEADS // KEY_VALUE_HEADS
    score_scale = 1.0 / math.sqrt(HEAD_WIDTH)
    positions = jnp.arange(PREFIX_SLOT_COUNT + PROMPT_TOKENS, dtype=jnp.int32)
    is_cache = positions < PREFIX_SLOT_COUNT
    span_index = positions - PREFIX_SLOT_COUNT

    def block_scores(block_index):
        row_start = (block_index * block_of_rows).astype(jnp.int32)
        picked_rows = lax.dynamic_slice_in_dim(queries, row_start, block_of_rows, 0)
        query_matrix = picked_rows.astype(jnp.float32).reshape(block_of_rows, KEY_VALUE_HEADS, head_group, HEAD_WIDTH)
        scores = jnp.einsum('bgrd,kgd->bgrk', query_matrix, key_matrix) * score_scale
        query_index = row_start + jnp.arange(block_of_rows, dtype=jnp.int32)
        visible = jnp.where(is_cache[None, :], positions[None, :] < prefix, span_index[None, :] <= query_index[:, None])
        visible = visible[:, None, None, :]
        row_peak = lax.optimization_barrier(jnp.max(jnp.where(visible, scores, masked_floor), axis=-1, keepdims=True))
        exponent = jnp.where(visible, jnp.exp(scores - row_peak), 0.0)
        row_total = lax.optimization_barrier(jnp.sum(exponent, axis=-1))
        weights = lax.optimization_barrier(exponent.astype(jnp.bfloat16)).astype(jnp.float32)
        weighted = jnp.einsum('bgrk,kgd->bgrd', weights, value_matrix)
        return (weighted / row_total[..., None]).reshape(block_of_rows, QUERY_HEADS * HEAD_WIDTH).astype(jnp.bfloat16)
    blocks = lax.map(block_scores, jnp.arange(PROMPT_TOKENS // block_of_rows, dtype=jnp.int32))
    return blocks.reshape(PROMPT_TOKENS, QUERY_HEADS * HEAD_WIDTH)

def expert_part(normed, routes, route_weight, w_gate, w_up, w_down):
    blocks = PROMPT_TOKENS // TOK_DEV
    normed_blocks = normed.astype(jnp.float32).reshape(blocks, TOK_DEV, D)
    route_blocks = routes.reshape(blocks, TOK_DEV, TOP)
    weight_blocks = route_weight.reshape(blocks, TOK_DEV, TOP)
    slot_ids = jnp.arange(SLOTS, dtype=jnp.int32)

    def one_expert(operands):
        expert, gate_mat, up_mat, down_mat = operands
        route_hits = route_blocks == expert
        chosen = jnp.any(route_hits, axis=-1)
        gate_w = lax.optimization_barrier(jnp.sum(jnp.where(route_hits, weight_blocks, 0.0), axis=-1))
        slot_rank = jnp.cumsum(chosen.astype(jnp.int32), axis=-1) - 1
        onehot = ((slot_rank[:, None, :] == slot_ids[None, :, None]) & chosen[:, None, :]).astype(jnp.float32)
        packed = jnp.einsum('bst,btd->bsd', onehot, normed_blocks, precision=lax.Precision.HIGHEST)
        packed = packed.reshape(blocks * SLOTS, D).astype(jnp.bfloat16)
        gate_proj = jnp.dot(packed, gate_mat, preferred_element_type=jnp.float32)
        up_proj = jnp.dot(packed, up_mat, preferred_element_type=jnp.float32)
        activation = (jax.nn.silu(gate_proj) * up_proj).astype(jnp.bfloat16)
        down_proj = jnp.dot(activation, down_mat, preferred_element_type=jnp.float32).reshape(blocks, SLOTS, D)
        unpacked = jnp.einsum('bst,bsd->btd', onehot, down_proj, precision=lax.Precision.HIGHEST)
        return (unpacked * gate_w[..., None]).reshape(PROMPT_TOKENS, D)
    outputs = lax.map(one_expert, (jnp.arange(FLIGHT, dtype=jnp.int32), w_gate, w_up, w_down))
    return lax.optimization_barrier(jnp.sum(outputs, axis=0))

def reference(queries, fresh_keys, fresh_values, prefix_key_cache, prefix_value_cache, prefix_len, residual, out_proj, norm_gain, routes, route_weight, w_gate, w_up, w_down):
    key_matrix = jnp.concatenate([prefix_key_cache, fresh_keys], axis=0).astype(jnp.float32).reshape(PREFIX_SLOT_COUNT + PROMPT_TOKENS, KEY_VALUE_HEADS, HEAD_WIDTH)
    value_matrix = jnp.concatenate([prefix_value_cache, fresh_values], axis=0).astype(jnp.float32).reshape(PREFIX_SLOT_COUNT + PROMPT_TOKENS, KEY_VALUE_HEADS, HEAD_WIDTH)
    attended = attend(queries, key_matrix, value_matrix, prefix_len[0])
    hidden = (residual.astype(jnp.float32) + jnp.dot(attended, out_proj, preferred_element_type=jnp.float32)).astype(jnp.bfloat16)
    hidden_f = hidden.astype(jnp.float32)
    normed = (hidden_f * lax.rsqrt(lax.optimization_barrier(jnp.mean(hidden_f * hidden_f, axis=-1, keepdims=True)) + 1e-05) * norm_gain).astype(jnp.bfloat16)
    mixed = expert_part(normed, routes, route_weight, w_gate, w_up, w_down)
    return (hidden_f + mixed).astype(jnp.bfloat16)
```

```python
import functools
import math

import jax
import jax.numpy as jnp
from jax import lax
from jax.experimental import pallas as pl
from jax.experimental.pallas import tpu as pltpu
from jax.sharding import PartitionSpec as P

HEAD_WIDTH = 128
SLOTS = 3


masked_floor = -1e30


def on_device(
    queries,
    fresh_keys,
    fresh_values,
    prefix_key_cache,
    prefix_value_cache,
    prefix_len,
    residual,
    out_proj,
    norm_gain,
    routes,
    route_weight,
    w_gate,
    w_up,
    w_down,
):
    tok_dev = queries.shape[0]
    cache_dev = prefix_key_cache.shape[0]
    n_ctx = lax.axis_size("ctx")
    tokens = tok_dev * n_ctx
    heads_dev = queries.shape[1] // HEAD_WIDTH
    groups = prefix_key_cache.shape[1] // HEAD_WIDTH
    ratio_q = heads_dev // groups
    key_count = cache_dev + tok_dev
    score_scale = 1.0 / math.sqrt(HEAD_WIDTH)
    ctx_rank = lax.axis_index("ctx")
    key_matrix = jnp.concatenate([prefix_key_cache, fresh_keys], axis=0).reshape(
        key_count, groups, HEAD_WIDTH
    )
    value_matrix = jnp.concatenate([prefix_value_cache, fresh_values], axis=0).reshape(
        key_count, groups, HEAD_WIDTH
    )
    cache_live = ctx_rank * cache_dev + jnp.arange(cache_dev, dtype=jnp.int32) < prefix_len[0]
    span_index = ctx_rank * tok_dev + jnp.arange(tok_dev, dtype=jnp.int32)
    all_queries = lax.all_gather(queries, "ctx", axis=0, tiled=True)
    block_of_rows = min(512, tokens)
    block_count = tokens // block_of_rows

    def block_setup(block_index):
        row_start = block_index * block_of_rows
        query_matrix = all_queries.reshape(block_of_rows, groups, ratio_q, HEAD_WIDTH)
        scores = (
            jnp.einsum(
                "bgrd,kgd->bgrk", query_matrix, key_matrix, preferred_element_type=jnp.float32
            )
            * score_scale
        )
        query_index = row_start + jnp.arange(block_of_rows, dtype=jnp.int32)
        visible = jnp.concatenate(
            [
                jnp.broadcast_to(cache_live[None, :], (block_of_rows, cache_dev)),
                span_index[None, :] <= query_index[:, None],
            ],
            axis=1,
        )[:, None, None, :]
        return (scores, visible)

    def block_peaks(block_index):
        scores, visible = block_setup(block_index)
        return jnp.max(jnp.where(visible, scores, masked_floor), axis=-1).reshape(
            block_of_rows, heads_dev
        )

    local_peak = lax.map(block_peaks, jnp.arange(block_count, dtype=jnp.int32))
    global_peak = lax.pmax(local_peak, "ctx")

    def block_partials(operands):
        block_index, peak_rows = operands
        scores, visible = block_setup(block_index)
        peak_full = peak_rows.reshape(block_of_rows, groups, ratio_q)
        exponent = jnp.where(visible, jnp.exp(scores - peak_full[..., None]), 0.0)
        row_total = jnp.sum(exponent, axis=-1)
        weighted = jnp.einsum(
            "bgrk,kgd->bgrd",
            exponent.astype(jnp.bfloat16),
            value_matrix,
            preferred_element_type=jnp.float32,
        )
        return (
            weighted.reshape(block_of_rows, heads_dev, HEAD_WIDTH),
            row_total.reshape(block_of_rows, heads_dev),
        )

    weighted, row_total = lax.map(
        block_partials, (jnp.arange(block_count, dtype=jnp.int32), global_peak)
    )
    weighted = weighted.reshape(tokens, heads_dev, HEAD_WIDTH)
    row_total = row_total.reshape(tokens, heads_dev)
    got_weighted, got_total = (
        lax.all_to_all(
            weighted.reshape(n_ctx, tok_dev, heads_dev, HEAD_WIDTH),
            "ctx",
            split_axis=0,
            concat_axis=0,
            tiled=True,
        ),
        lax.all_to_all(
            row_total.reshape(n_ctx, tok_dev, heads_dev),
            "ctx",
            split_axis=0,
            concat_axis=0,
            tiled=True,
        ),
    )
    numer = jnp.sum(got_weighted, axis=0)
    denom = jnp.sum(got_total, axis=0)
    attended = (
        (numer / denom[..., None]).reshape(tok_dev, heads_dev * HEAD_WIDTH).astype(jnp.bfloat16)
    )
    projected = jnp.dot(
        lax.all_gather(attended, "ctx", axis=0, tiled=True),
        out_proj,
        preferred_element_type=jnp.float32,
    )
    col_dev = projected.shape[1]
    token_cols = lax.all_to_all(
        projected.reshape(n_ctx, tok_dev, col_dev), "ctx", split_axis=0, concat_axis=2, tiled=True
    )
    attn_rows = lax.psum(token_cols.reshape(tok_dev, n_ctx * col_dev), "exp")
    hidden = (residual.astype(jnp.float32) + attn_rows).astype(jnp.bfloat16)
    hidden_f = hidden.astype(jnp.float32)
    normed = (
        hidden_f
        * lax.rsqrt(jnp.mean(hidden_f * hidden_f, axis=-1, keepdims=True) + 1e-05)
        * norm_gain
    ).astype(jnp.bfloat16)
    expert = lax.axis_index("exp")
    route_hits = routes == expert
    chosen = jnp.any(route_hits, axis=-1)
    gate_w = jnp.sum(jnp.where(route_hits, route_weight, 0.0), axis=-1)
    slot_rank = jnp.cumsum(chosen.astype(jnp.int32)) - 1
    slot_ids = jnp.arange(SLOTS, dtype=jnp.int32)
    onehot = ((slot_rank[None, :] == slot_ids[:, None]) & chosen[None, :]).astype(jnp.bfloat16)
    packed = jnp.dot(onehot, normed, preferred_element_type=jnp.float32).astype(jnp.bfloat16)
    gate_mat = w_gate[0]
    up_mat = w_up[0]
    down_mat = w_down[0]
    shard_rows = lax.all_gather(packed, "ctx", axis=0, tiled=True)
    gate_proj = jnp.dot(shard_rows, gate_mat, preferred_element_type=jnp.float32)
    up_proj = jnp.dot(shard_rows, up_mat, preferred_element_type=jnp.float32)
    activation = (jax.nn.silu(gate_proj) * up_proj).astype(jnp.bfloat16)
    own_sums = lax.psum_scatter(
        jnp.dot(activation, down_mat, preferred_element_type=jnp.float32),
        "ctx",
        scatter_dimension=0,
        tiled=True,
    )
    unpacked = jnp.dot(onehot.astype(jnp.float32).T, own_sums, precision=lax.Precision.HIGHEST)
    mixed = lax.psum(unpacked * gate_w[:, None], "exp")
    return (hidden_f + mixed).astype(jnp.bfloat16)


MESH_FLOOR = -1e30
NT = (((1,), (1,)), ((), ()))
PIECES = 3


def layer_kernel(
    n, plen_ref, q_ref, fk_ref, fv_ref, k_ref, v_ref, res_ref, gain_ref, routes_ref, rw_ref,
    op_hbm, wg_hbm, wu_hbm, wd_hbm, out_ref,
    w_v, wd_v, op_v, qs, qg, info_s, info_g, rs, rg, os_, og, ss, sg, ats, atg, ps, pr,
    hs, hg, xs, xg, normed, acc, spread, ys, yg, total, ms, mr,
    lsem, send, recv, psend, precv,
):
    f32, bf16 = jnp.float32, jnp.bfloat16
    me = lax.axis_index("ctx")
    expert = lax.axis_index("exp")
    tok, width = res_ref.shape
    cols = width // n
    half = cols // 2
    head_count = q_ref.shape[1] // HEAD_WIDTH
    groups = k_ref.shape[1] // HEAD_WIDTH
    ratio = head_count // groups
    rows_g = ratio * tok
    cache = k_ref.shape[0]
    tokens = n * tok
    packed_rows = n * SLOTS
    ff = wg_hbm.shape[1]
    piece = width // PIECES
    tiles = piece // 128
    wd_half = ff // 2

    op_copy = pltpu.make_async_copy(op_hbm, op_v, lsem.at[0])
    op_copy.start()

    def gate_copy(j):
        return pltpu.make_async_copy(
            wg_hbm.at[pl.ds(j * cols, cols), :], w_v.at[pl.ds(j * cols, cols), :], lsem.at[1 + j]
        )

    def up_copy(j):
        return pltpu.make_async_copy(
            wu_hbm.at[pl.ds(j * cols, cols), :],
            w_v.at[pl.ds(width + j * cols, cols), :],
            lsem.at[1 + n + j],
        )

    def down_copy(i):
        p, h = i // 2, i % 2
        src = wd_hbm.at[pl.ds(h * wd_half, wd_half), pl.ds(p * piece, piece)]
        dst = wd_v if i == 0 else w_v.at[pl.ds((i - 1) * wd_half, wd_half), :]
        return pltpu.make_async_copy(src, dst, lsem.at[1 + 2 * n + i])

    def each(body, first=0):
        def step(k, c):
            body(lax.rem(me + k, n))
            return c

        lax.fori_loop(first, n, step, 0)

    each(lambda j: gate_copy(j).start())
    each(lambda j: up_copy(j).start())
    down_copy(0).start()

    barrier = pltpu.get_barrier_semaphore()

    def greet(d):
        pl.semaphore_signal(
            barrier, inc=1, device_id={"ctx": d}, device_id_type=pl.DeviceIdType.MESH
        )

    each(greet, 1)
    pl.semaphore_signal(
        barrier, inc=1, device_id={"exp": 1 - expert}, device_id_type=pl.DeviceIdType.MESH
    )

    def remote(phase, src, dst, d, slot):
        return pltpu.make_async_remote_copy(
            src_ref=src, dst_ref=dst, send_sem=send.at[phase, d], recv_sem=recv.at[phase, slot],
            device_id={"ctx": d}, device_id_type=pl.DeviceIdType.MESH,
        )

    def scatter(phase, src_of, dst):
        each(lambda d: remote(phase, src_of(d), dst.at[me], d, me).start(), 1)

    def arrived(phase, dst, i):
        remote(phase, dst.at[i], dst.at[i], i, i).wait_recv()

    def gathered(phase, dst):
        each(lambda i: arrived(phase, dst, i), 1)

    def partner(i, src, dst):
        return pltpu.make_async_remote_copy(
            src_ref=src, dst_ref=dst, send_sem=psend.at[i], recv_sem=precv.at[i],
            device_id={"exp": 1 - expert}, device_id_type=pl.DeviceIdType.MESH,
        )

    q = q_ref[...].astype(f32)
    qv = jnp.concatenate(
        [q[:, h * HEAD_WIDTH : (h + 1) * HEAD_WIDTH] for h in range(head_count)], axis=0
    ).astype(bf16)
    qs[...] = qv
    qg[me] = qv

    hit = (routes_ref[...] == expert).astype(f32)
    chosen = jnp.max(hit, axis=1, keepdims=True)
    gate_w = jnp.sum(hit * rw_ref[...], axis=1, keepdims=True)
    lane = lax.broadcasted_iota(jnp.int32, (tok, 128), 1)
    sub = lax.broadcasted_iota(jnp.int32, (tok, 128), 0)
    chosen_row = jnp.sum(jnp.where(lane == sub, chosen, 0.0), axis=0, keepdims=True)
    rank = jnp.sum(jnp.where(lane < sub, chosen_row, 0.0), axis=1, keepdims=True)
    slot1 = jnp.where(chosen > 0.0, rank + 1.0, 0.0)
    slot_row = jnp.sum(jnp.where(lane == sub + me * tok, slot1, 0.0), axis=0, keepdims=True)
    info = jnp.broadcast_to(slot_row, (8, 128))
    info_s[...] = info
    info_g[me] = info

    res = res_ref[...].astype(f32)
    for j in range(n):
        block = res[:, j * cols : (j + 1) * cols]
        rs[j] = jnp.concatenate([block[:, :half], block[:, half:]], axis=0).astype(bf16)
    ss[...] = jnp.zeros_like(ss)

    pl.semaphore_wait(barrier, n)
    scatter(0, lambda d: qs, qg)
    scatter(1, lambda d: info_s, info_g)
    scatter(2, lambda d: rs.at[d], rg)
    rg[me] = rs[me]

    gathered(0, qg)
    prefix = plen_ref[0]
    pad = jnp.zeros((128 - tok, groups * HEAD_WIDTH), f32)
    fk = jnp.concatenate([fk_ref[...].astype(f32), pad], axis=0).astype(bf16)
    fv = jnp.concatenate([fv_ref[...].astype(f32), pad], axis=0).astype(bf16)
    rows = n * rows_g
    cache_live = me * cache + lax.broadcasted_iota(jnp.int32, (1, cache), 1) < prefix
    row_token = lax.broadcasted_iota(jnp.int32, (n, rows_g, 128), 0) * tok + (
        lax.broadcasted_iota(jnp.int32, (n, rows_g, 128), 1) & (tok - 1)
    )
    key_lane = lax.broadcasted_iota(jnp.int32, (n, rows_g, 128), 2)
    fresh_live = jnp.where(
        (key_lane < tok) & (me * tok + key_lane <= row_token), 1, 0
    ).reshape(rows, 128) > 0
    eye = lax.broadcasted_iota(jnp.int32, (1, rows_g, 128), 1) == lax.broadcasted_iota(
        jnp.int32, (1, rows_g, 128), 2
    )
    score_scale = 1.0 / math.sqrt(HEAD_WIDTH)
    for g in range(groups):
        lo, hi = g * HEAD_WIDTH, (g + 1) * HEAD_WIDTH
        qm = qg[:, g * rows_g : (g + 1) * rows_g, :].reshape(rows, HEAD_WIDTH)
        s1 = lax.dot_general(qm, k_ref[:, lo:hi], NT, preferred_element_type=f32) * score_scale
        s2 = lax.dot_general(qm, fk[:, lo:hi], NT, preferred_element_type=f32) * score_scale
        s1 = jnp.where(cache_live, s1, MESH_FLOOR)
        s2 = jnp.where(fresh_live, s2, MESH_FLOOR)
        peak = jnp.maximum(
            jnp.max(s1, axis=1, keepdims=True), jnp.max(s2, axis=1, keepdims=True)
        )
        e1 = jnp.where(cache_live, jnp.exp(s1 - peak), 0.0)
        e2 = jnp.where(fresh_live, jnp.exp(s2 - peak), 0.0)
        part = jnp.sum(e1, axis=1, keepdims=True) + jnp.sum(e2, axis=1, keepdims=True)
        o = jnp.dot(e1.astype(bf16), v_ref[:, lo:hi], preferred_element_type=f32) + jnp.dot(
            e2.astype(bf16), fv[:, lo:hi], preferred_element_type=f32
        )
        safe = jnp.maximum(part, 1e-30)
        lse = jnp.where(part > 0.0, peak + jnp.log(safe), MESH_FLOOR)
        os_[:, g * rows_g : (g + 1) * rows_g, :] = (
            (o / safe).astype(bf16).reshape(n, rows_g, HEAD_WIDTH)
        )
        ss[:, g : g + 1, :] = jnp.sum(
            jnp.where(eye, lse.reshape(n, rows_g, 1), 0.0), axis=1, keepdims=True
        )
    scatter(4, lambda d: ss.at[d], sg)
    scatter(3, lambda d: os_.at[d], og)
    og[me] = os_[me]
    sg[me] = ss[me]

    gathered(4, sg)
    gathered(3, og)
    for g in range(groups):
        stat = sg[:, g : g + 1, :]
        share = jnp.exp(stat - jnp.max(stat, axis=0, keepdims=True))
        share = share / jnp.sum(share, axis=0, keepdims=True)
        share = jnp.sum(jnp.where(eye, share, 0.0), axis=2, keepdims=True)
        part_o = og[:, g * rows_g : (g + 1) * rows_g, :].astype(f32)
        ats[g * rows_g : (g + 1) * rows_g, :] = jnp.sum(share * part_o, axis=0).astype(bf16)
    scatter(5, lambda d: ats, atg)
    atg[me] = ats[...]
    gathered(5, atg)
    af = atg[...].astype(f32)
    attended = jnp.concatenate(
        [af[:, h * tok : (h + 1) * tok, :].reshape(tokens, HEAD_WIDTH) for h in range(head_count)],
        axis=1,
    ).astype(bf16)
    op_copy.wait()
    proj = jnp.dot(attended, op_v[...], preferred_element_type=f32)
    ps[...] = proj
    swap = partner(0, ps, pr)
    swap.start()
    gathered(1, info_g)
    gathered(2, rg)
    rf = rg[...].astype(f32)
    resid = jnp.concatenate(
        [rf[:, :tok, :].reshape(tokens, half), rf[:, tok:, :].reshape(tokens, half)], axis=1
    )
    slot_all = jnp.sum(info_g[:, 0:1, :], axis=0).astype(jnp.int32)
    lane_p = lax.broadcasted_iota(jnp.int32, (packed_rows, 128), 1)
    row_p = lax.broadcasted_iota(jnp.int32, (packed_rows, 128), 0)
    place = (lane_p >> 3) * SLOTS + slot_all - 1
    select = jnp.where((row_p == place) & (slot_all > 0), 1.0, 0.0)[:, :tokens].astype(bf16)
    swap.wait_recv()
    hidden = (resid + (proj + pr[...])).astype(bf16)
    hp = jnp.dot(select, hidden, preferred_element_type=f32)
    hv = jnp.concatenate([hp[:, :half], hp[:, half:]], axis=0).astype(bf16)
    hs[...] = hv
    hg[me] = hv
    scatter(6, lambda d: hs, hg)
    hf = hidden.astype(f32)
    for j in range(n):
        block = hf[j * tok : (j + 1) * tok, :]
        xs[j] = jnp.concatenate([block[:, :half], block[:, half:]], axis=0).astype(bf16)
    scatter(7, lambda d: xs.at[d], xg)
    xg[me] = xs[me]

    col_tile = 512
    acc[...] = jnp.zeros_like(acc)

    def gate_step(k, squares):
        j = lax.rem(me + k, n)

        @pl.when(k > 0)
        def _():
            arrived(6, hg, j)

        hb = hg[j].astype(f32)
        x = jnp.concatenate([hb[:packed_rows], hb[packed_rows:]], axis=1)
        xb = (x * gain_ref[j]).astype(bf16)
        normed[j] = xb
        gate_copy(j).wait()

        def tile(c, z):
            at = pl.ds(pl.multiple_of(c * col_tile, col_tile), col_tile)
            w = w_v[pl.ds(pl.multiple_of(j * cols, cols), cols), at]
            acc[0, :, at] += jnp.dot(xb, w, preferred_element_type=f32)
            return z

        lax.fori_loop(0, ff // col_tile, tile, 0)
        return squares + jnp.sum(x * x, axis=1, keepdims=True)

    squares = lax.fori_loop(0, n, gate_step, jnp.zeros((packed_rows, 1), f32))
    for i in range(1, 2 * PIECES):
        down_copy(i).start()

    def up_step(k, z):
        j = lax.rem(me + k, n)
        up_copy(j).wait()
        xb = normed[j]

        def tile(c, y):
            at = pl.ds(pl.multiple_of(c * col_tile, col_tile), col_tile)
            w = w_v[pl.ds(pl.multiple_of(width + j * cols, cols), cols), at]
            acc[1, :, at] += jnp.dot(xb, w, preferred_element_type=f32)
            return y

        lax.fori_loop(0, ff // col_tile, tile, 0)
        return z

    lax.fori_loop(0, n, up_step, 0)
    factor = lax.rsqrt(squares / width + 1e-5)
    gate = acc[0] * factor
    up = acc[1] * factor
    act = (gate / (1.0 + jnp.exp(-gate)) * up).astype(bf16)

    for p in range(PIECES):
        down_copy(2 * p).wait()
        down_copy(2 * p + 1).wait()
        for c in range(piece // col_tile):
            at = slice(c * col_tile, (c + 1) * col_tile)
            first = wd_v[:, at] if p == 0 else w_v[(2 * p - 1) * wd_half : 2 * p * wd_half, at]
            second = w_v[2 * p * wd_half : (2 * p + 1) * wd_half, at]
            d = jnp.dot(act[:, :wd_half], first, preferred_element_type=f32)
            d += jnp.dot(act[:, wd_half:], second, preferred_element_type=f32)
            for t in range(col_tile // 128):
                spread[pl.ds(c * (col_tile // 128) + t, packed_rows, stride=tiles), :] = d[
                    :, t * 128 : (t + 1) * 128
                ]
        ys[p] = spread[...].astype(bf16).reshape(n, SLOTS * tiles, 128)
        yg[p, me] = ys[p, me]
        scatter(8 + p, lambda d: ys.at[p, d], yg.at[p])

    swaps = []
    for p in range(PIECES):
        gathered(8 + p, yg.at[p])
        total[p] = jnp.sum(yg[p].astype(f32), axis=0)
        for t in range(tiles):
            mixed = jnp.zeros((tok, 128), f32)
            for s in range(SLOTS):
                weight = jnp.where(slot1 == s + 1.0, gate_w, 0.0)
                mixed += weight * total[p, s * tiles + t : s * tiles + t + 1, :]
            ms[p, :, t * 128 : (t + 1) * 128] = mixed
        swaps.append(partner(1 + p, ms.at[p], mr.at[p]))
        swaps[-1].start()
    gathered(7, xg)
    own = []
    for j in range(n):
        block = xg[j].astype(f32)
        own.append(jnp.concatenate([block[:tok], block[tok:]], axis=1))
    own = jnp.concatenate(own, axis=1)
    for p in range(PIECES):
        swaps[p].wait_recv()
        at = slice(p * piece, (p + 1) * piece)
        out_ref[:, at] = (own[:, at] + (ms[p] + mr[p])).astype(bf16)

    def sent(phase, src):
        each(lambda d: remote(phase, src(d), src(d), d, d).wait_send(), 1)

    sent(0, lambda d: qs)
    sent(1, lambda d: info_s)
    sent(2, lambda d: rs.at[d])
    sent(3, lambda d: os_.at[d])
    sent(4, lambda d: ss.at[d])
    sent(5, lambda d: ats)
    sent(6, lambda d: hs)
    sent(7, lambda d: xs.at[d])
    for p in range(PIECES):
        sent(8 + p, lambda d: ys.at[p, d])
    swap.wait_send()
    for s in swaps:
        s.wait_send()


def one_kernel(
    queries, fresh_keys, fresh_values, prefix_key_cache, prefix_value_cache, prefix_len,
    residual, out_proj, norm_gain, routes, route_weight, w_gate, w_up, w_down,
):
    n = lax.axis_size("ctx")
    tok, width = residual.shape
    cols = width // n
    half = cols // 2
    head_rows = queries.shape[1] // HEAD_WIDTH * tok
    tokens = n * tok
    ff = w_gate.shape[2]
    piece = width // PIECES
    prow = n * SLOTS
    f32, bf16 = jnp.float32, jnp.bfloat16
    V = pltpu.VMEM
    vmem = pl.BlockSpec(memory_space=pltpu.VMEM)
    hbm = pl.BlockSpec(memory_space=pl.ANY)
    return pl.pallas_call(
        functools.partial(layer_kernel, n),
        out_shape=jax.ShapeDtypeStruct(residual.shape, bf16),
        in_specs=[pl.BlockSpec(memory_space=pltpu.SMEM)] + [vmem] * 9 + [hbm] * 4,
        out_specs=vmem,
        scratch_shapes=[
            V((2 * width, ff), bf16),
            V((ff // 2, piece), bf16),
            V(out_proj.shape, bf16),
            V((head_rows, HEAD_WIDTH), bf16),
            V((n, head_rows, HEAD_WIDTH), bf16),
            V((8, 128), f32),
            V((n, 8, 128), f32),
            V((n, 2 * tok, half), bf16),
            V((n, 2 * tok, half), bf16),
            V((n, head_rows, HEAD_WIDTH), bf16),
            V((n, head_rows, HEAD_WIDTH), bf16),
            V((n, 8, 128), f32),
            V((n, 8, 128), f32),
            V((head_rows, HEAD_WIDTH), bf16),
            V((n, head_rows, HEAD_WIDTH), bf16),
            V((tokens, cols), f32),
            V((tokens, cols), f32),
            V((2 * prow, half), bf16),
            V((n, 2 * prow, half), bf16),
            V((n, 2 * tok, half), bf16),
            V((n, 2 * tok, half), bf16),
            V((n, prow, cols), bf16),
            V((2, prow, ff), f32),
            V((prow * (piece // 128), 128), f32),
            V((PIECES, n, SLOTS * (piece // 128), 128), bf16),
            V((PIECES, n, SLOTS * (piece // 128), 128), bf16),
            V((PIECES, SLOTS * (piece // 128), 128), f32),
            V((PIECES, tok, piece), f32),
            V((PIECES, tok, piece), f32),
            pltpu.SemaphoreType.DMA((1 + 2 * n + 2 * PIECES,)),
            pltpu.SemaphoreType.DMA((8 + PIECES, n)),
            pltpu.SemaphoreType.DMA((8 + PIECES, n)),
            pltpu.SemaphoreType.DMA((1 + PIECES,)),
            pltpu.SemaphoreType.DMA((1 + PIECES,)),
        ],
        compiler_params=pltpu.CompilerParams(
            collective_id=0, has_side_effects=True, vmem_limit_bytes=63 * 2**20
        ),
        name="prefill_layer",
    )(
        prefix_len, queries, fresh_keys, fresh_values, prefix_key_cache, prefix_value_cache,
        residual, norm_gain.reshape(n, 1, cols), routes, route_weight, out_proj,
        w_gate.reshape(w_gate.shape[1:]), w_up.reshape(w_up.shape[1:]),
        w_down.reshape(w_down.shape[1:]),
    )


def layer(*args):
    queries, w_gate, residual = args[0], args[11], args[6]
    n = lax.axis_size("ctx")
    tokens = n * residual.shape[0]
    width, ff = w_gate.shape[1:]
    fits = tokens <= 128 and residual.shape[0] == 8 and width == PIECES * ff
    fits = fits and width % (n * 256) == 0 and lax.axis_size("exp") == 2
    return one_kernel(*args) if fits else on_device(*args)


def solution(mesh):
    return jax.shard_map(
        layer,
        mesh=mesh,
        in_specs=(
            P(("grp", "ctx"), "exp"),
            P(("grp", "ctx"), "exp"),
            P(("grp", "ctx"), "exp"),
            P(("grp", "ctx"), "exp"),
            P(("grp", "ctx"), "exp"),
            P("grp"),
            P(("grp", "ctx"), None),
            P("exp", "ctx"),
            P(),
            P(("grp", "ctx"), None),
            P(("grp", "ctx"), None),
            P("exp", None, "ctx"),
            P("exp", None, "ctx"),
            P("exp", "ctx", None),
        ),
        out_specs=P(("grp", "ctx"), None),
        check_vma=False,
    )
```

```python
import functools
import math

import jax
import jax.numpy as jnp
from jax import lax
from jax.experimental import pallas as pl
from jax.experimental.pallas import tpu as pltpu
from jax.sharding import PartitionSpec as P

HEAD_WIDTH = 128
SLOTS = 3


masked_floor = -1e30


def on_device(
    queries,
    fresh_keys,
    fresh_values,
    prefix_key_cache,
    prefix_value_cache,
    prefix_len,
    residual,
    out_proj,
    norm_gain,
    routes,
    route_weight,
    w_gate,
    w_up,
    w_down,
):
    tok_dev = queries.shape[0]
    cache_dev = prefix_key_cache.shape[0]
    n_ctx = lax.axis_size("ctx")
    tokens = tok_dev * n_ctx
    heads_dev = queries.shape[1] // HEAD_WIDTH
    groups = prefix_key_cache.shape[1] // HEAD_WIDTH
    ratio_q = heads_dev // groups
    key_count = cache_dev + tok_dev
    score_scale = 1.0 / math.sqrt(HEAD_WIDTH)
    ctx_rank = lax.axis_index("ctx")
    key_matrix = jnp.concatenate([prefix_key_cache, fresh_keys], axis=0).reshape(
        key_count, groups, HEAD_WIDTH
    )
    value_matrix = jnp.concatenate([prefix_value_cache, fresh_values], axis=0).reshape(
        key_count, groups, HEAD_WIDTH
    )
    cache_live = ctx_rank * cache_dev + jnp.arange(cache_dev, dtype=jnp.int32) < prefix_len[0]
    span_index = ctx_rank * tok_dev + jnp.arange(tok_dev, dtype=jnp.int32)
    all_queries = lax.all_gather(queries, "ctx", axis=0, tiled=True)
    block_of_rows = min(512, tokens)
    block_count = tokens // block_of_rows

    def block_setup(block_index):
        row_start = block_index * block_of_rows
        query_matrix = all_queries.reshape(block_of_rows, groups, ratio_q, HEAD_WIDTH)
        scores = (
            jnp.einsum(
                "bgrd,kgd->bgrk", query_matrix, key_matrix, preferred_element_type=jnp.float32
            )
            * score_scale
        )
        query_index = row_start + jnp.arange(block_of_rows, dtype=jnp.int32)
        visible = jnp.concatenate(
            [
                jnp.broadcast_to(cache_live[None, :], (block_of_rows, cache_dev)),
                span_index[None, :] <= query_index[:, None],
            ],
            axis=1,
        )[:, None, None, :]
        return (scores, visible)

    def block_peaks(block_index):
        scores, visible = block_setup(block_index)
        return jnp.max(jnp.where(visible, scores, masked_floor), axis=-1).reshape(
            block_of_rows, heads_dev
        )

    local_peak = lax.map(block_peaks, jnp.arange(block_count, dtype=jnp.int32))
    global_peak = lax.pmax(local_peak, "ctx")

    def block_partials(operands):
        block_index, peak_rows = operands
        scores, visible = block_setup(block_index)
        peak_full = peak_rows.reshape(block_of_rows, groups, ratio_q)
        exponent = jnp.where(visible, jnp.exp(scores - peak_full[..., None]), 0.0)
        row_total = jnp.sum(exponent, axis=-1)
        weighted = jnp.einsum(
            "bgrk,kgd->bgrd",
            exponent.astype(jnp.bfloat16),
            value_matrix,
            preferred_element_type=jnp.float32,
        )
        return (
            weighted.reshape(block_of_rows, heads_dev, HEAD_WIDTH),
            row_total.reshape(block_of_rows, heads_dev),
        )

    weighted, row_total = lax.map(
        block_partials, (jnp.arange(block_count, dtype=jnp.int32), global_peak)
    )
    weighted = weighted.reshape(tokens, heads_dev, HEAD_WIDTH)
    row_total = row_total.reshape(tokens, heads_dev)
    got_weighted, got_total = (
        lax.all_to_all(
            weighted.reshape(n_ctx, tok_dev, heads_dev, HEAD_WIDTH),
            "ctx",
            split_axis=0,
            concat_axis=0,
            tiled=True,
        ),
        lax.all_to_all(
            row_total.reshape(n_ctx, tok_dev, heads_dev),
            "ctx",
            split_axis=0,
            concat_axis=0,
            tiled=True,
        ),
    )
    numer = jnp.sum(got_weighted, axis=0)
    denom = jnp.sum(got_total, axis=0)
    attended = (
        (numer / denom[..., None]).reshape(tok_dev, heads_dev * HEAD_WIDTH).astype(jnp.bfloat16)
    )
    projected = jnp.dot(
        lax.all_gather(attended, "ctx", axis=0, tiled=True),
        out_proj,
        preferred_element_type=jnp.float32,
    )
    col_dev = projected.shape[1]
    token_cols = lax.all_to_all(
        projected.reshape(n_ctx, tok_dev, col_dev), "ctx", split_axis=0, concat_axis=2, tiled=True
    )
    attn_rows = lax.psum(token_cols.reshape(tok_dev, n_ctx * col_dev), "exp")
    hidden = (residual.astype(jnp.float32) + attn_rows).astype(jnp.bfloat16)
    hidden_f = hidden.astype(jnp.float32)
    normed = (
        hidden_f
        * lax.rsqrt(jnp.mean(hidden_f * hidden_f, axis=-1, keepdims=True) + 1e-05)
        * norm_gain
    ).astype(jnp.bfloat16)
    expert = lax.axis_index("exp")
    route_hits = routes == expert
    chosen = jnp.any(route_hits, axis=-1)
    gate_w = jnp.sum(jnp.where(route_hits, route_weight, 0.0), axis=-1)
    slot_rank = jnp.cumsum(chosen.astype(jnp.int32)) - 1
    slot_ids = jnp.arange(SLOTS, dtype=jnp.int32)
    onehot = ((slot_rank[None, :] == slot_ids[:, None]) & chosen[None, :]).astype(jnp.bfloat16)
    packed = jnp.dot(onehot, normed, preferred_element_type=jnp.float32).astype(jnp.bfloat16)
    gate_mat = w_gate[0]
    up_mat = w_up[0]
    down_mat = w_down[0]
    shard_rows = lax.all_gather(packed, "ctx", axis=0, tiled=True)
    gate_proj = jnp.dot(shard_rows, gate_mat, preferred_element_type=jnp.float32)
    up_proj = jnp.dot(shard_rows, up_mat, preferred_element_type=jnp.float32)
    activation = (jax.nn.silu(gate_proj) * up_proj).astype(jnp.bfloat16)
    own_sums = lax.psum_scatter(
        jnp.dot(activation, down_mat, preferred_element_type=jnp.float32),
        "ctx",
        scatter_dimension=0,
        tiled=True,
    )
    unpacked = jnp.dot(onehot.astype(jnp.float32).T, own_sums, precision=lax.Precision.HIGHEST)
    mixed = lax.psum(unpacked * gate_w[:, None], "exp")
    return (hidden_f + mixed).astype(jnp.bfloat16)


MESH_FLOOR = -1e30
NT = (((1,), (1,)), ((), ()))
PIECES = 3


def layer_kernel(
    n, plen_ref, q_ref, fk_ref, fv_ref, k_ref, v_ref, res_ref, gain_ref, routes_ref, rw_ref,
    op_hbm, wg_hbm, wu_hbm, wd_hbm, out_ref,
    w_v, wd_v, op_v, qs, qg, info_s, info_g, rs, rg, os_, og, ats, atg, ps, pr,
    hs, hg, xs, xg, normed, acc, spread, ys, yg, total, ms, mr,
    lsem, send, recv, psend, precv,
):
    f32, bf16 = jnp.float32, jnp.bfloat16
    me = lax.axis_index("ctx")
    expert = lax.axis_index("exp")
    tok, width = res_ref.shape
    cols = width // n
    half = cols // 2
    head_count = q_ref.shape[1] // HEAD_WIDTH
    groups = k_ref.shape[1] // HEAD_WIDTH
    ratio = head_count // groups
    rows_g = ratio * tok
    cache = k_ref.shape[0]
    tokens = n * tok
    packed_rows = n * SLOTS
    ff = wg_hbm.shape[1]
    piece = width // PIECES
    tiles = piece // 128
    wd_half = ff // 2

    op_copy = pltpu.make_async_copy(op_hbm, op_v, lsem.at[0])
    op_copy.start()

    def gate_copy(j):
        return pltpu.make_async_copy(
            wg_hbm.at[pl.ds(j * cols, cols), :], w_v.at[pl.ds(j * cols, cols), :], lsem.at[1 + j]
        )

    def up_copy(j):
        return pltpu.make_async_copy(
            wu_hbm.at[pl.ds(j * cols, cols), :],
            w_v.at[pl.ds(width + j * cols, cols), :],
            lsem.at[1 + n + j],
        )

    def down_copy(i):
        p, h = i // 2, i % 2
        src = wd_hbm.at[pl.ds(h * wd_half, wd_half), pl.ds(p * piece, piece)]
        dst = wd_v if i == 0 else w_v.at[pl.ds((i - 1) * wd_half, wd_half), :]
        return pltpu.make_async_copy(src, dst, lsem.at[1 + 2 * n + i])

    def each(body, first=0):
        def step(k, c):
            body(lax.rem(me + k, n))
            return c

        lax.fori_loop(first, n, step, 0)

    each(lambda j: gate_copy(j).start())
    each(lambda j: up_copy(j).start())
    down_copy(0).start()

    barrier = pltpu.get_barrier_semaphore()

    def greet(d):
        pl.semaphore_signal(
            barrier, inc=1, device_id={"ctx": d}, device_id_type=pl.DeviceIdType.MESH
        )

    each(greet, 1)
    pl.semaphore_signal(
        barrier, inc=1, device_id={"exp": 1 - expert}, device_id_type=pl.DeviceIdType.MESH
    )

    def remote(phase, src, dst, d, slot):
        return pltpu.make_async_remote_copy(
            src_ref=src, dst_ref=dst, send_sem=send.at[phase, d], recv_sem=recv.at[phase, slot],
            device_id={"ctx": d}, device_id_type=pl.DeviceIdType.MESH,
        )

    def scatter(phase, src_of, dst_of):
        each(lambda d: remote(phase, src_of(d), dst_of(me), d, me).start(), 1)

    def arrived(phase, dst_of, i):
        remote(phase, dst_of(i), dst_of(i), i, i).wait_recv()

    def gathered(phase, dst_of):
        each(lambda i: arrived(phase, dst_of, i), 1)

    def partner(i, src, dst):
        return pltpu.make_async_remote_copy(
            src_ref=src, dst_ref=dst, send_sem=psend.at[i], recv_sem=precv.at[i],
            device_id={"exp": 1 - expert}, device_id_type=pl.DeviceIdType.MESH,
        )

    q = q_ref[...].astype(f32)
    qv = jnp.concatenate(
        [q[:, h * HEAD_WIDTH : (h + 1) * HEAD_WIDTH] for h in range(head_count)], axis=0
    ).astype(bf16)
    qs[...] = qv
    qg[me] = qv

    hit = (routes_ref[...] == expert).astype(f32)
    chosen_row = jnp.max(hit, axis=0, keepdims=True)
    weight_row = jnp.sum(hit * rw_ref[...], axis=0, keepdims=True)
    lane_t = lax.broadcasted_iota(jnp.int32, (tok, tok), 1)
    sub_t = lax.broadcasted_iota(jnp.int32, (tok, tok), 0)

    def column(keep, row):
        return jnp.sum(jnp.where(keep, row, 0.0), axis=1, keepdims=True)

    chosen = column(lane_t == sub_t, chosen_row)
    gate_w = column(lane_t == sub_t, weight_row)
    rank = column(lane_t < sub_t, chosen_row)
    slot1 = jnp.where(chosen > 0.0, rank + 1.0, 0.0)
    lane = lax.broadcasted_iota(jnp.int32, (tok, 128), 1)
    sub = lax.broadcasted_iota(jnp.int32, (tok, 128), 0)
    slot_row = jnp.sum(jnp.where(lane == sub + me * tok, slot1, 0.0), axis=0, keepdims=True)
    info = jnp.broadcast_to(slot_row, (8, 128))
    info_s[...] = info
    info_g[me] = info

    res = res_ref[...].astype(f32)
    for j in range(n):
        block = res[:, j * cols : (j + 1) * cols]
        rs[j] = jnp.concatenate([block[:, :half], block[:, half:]], axis=0).astype(bf16)

    pl.semaphore_wait(barrier, n)
    for g in range(groups):
        part = pl.ds(g * rows_g, rows_g)
        scatter(g, lambda d: qs.at[part], lambda i: qg.at[i, part])
    scatter(6, lambda d: info_s, lambda i: info_g.at[i])
    scatter(7, lambda d: rs.at[d], lambda i: rg.at[i])
    rg[me] = rs[me]

    prefix = plen_ref[0]
    pad = jnp.zeros((128 - tok, groups * HEAD_WIDTH), f32)
    fk = jnp.concatenate([fk_ref[...].astype(f32), pad], axis=0).astype(bf16)
    fv = jnp.concatenate([fv_ref[...].astype(f32), pad], axis=0).astype(bf16)
    rows = n * rows_g
    cache_live = me * cache + lax.broadcasted_iota(jnp.int32, (1, cache), 1) < prefix
    row_token = lax.broadcasted_iota(jnp.int32, (n, rows_g, 128), 0) * tok + (
        lax.broadcasted_iota(jnp.int32, (n, rows_g, 128), 1) & (tok - 1)
    )
    key_lane = lax.broadcasted_iota(jnp.int32, (n, rows_g, 128), 2)
    fresh_live = jnp.where(
        (key_lane < tok) & (me * tok + key_lane <= row_token), 1, 0
    ).reshape(rows, 128) > 0
    eye = lax.broadcasted_iota(jnp.int32, (1, rows_g, 128), 1) == lax.broadcasted_iota(
        jnp.int32, (1, rows_g, 128), 2
    )
    score_scale = 1.0 / math.sqrt(HEAD_WIDTH)
    term = lax.broadcasted_iota(jnp.int32, (n, 16, 128), 1)
    for g in range(groups):
        lo, hi = g * HEAD_WIDTH, (g + 1) * HEAD_WIDTH
        part = pl.ds(g * rows_g, rows_g)
        gathered(g, lambda i: qg.at[i, part])
        qm = qg[:, g * rows_g : (g + 1) * rows_g, :].reshape(rows, HEAD_WIDTH)
        s1 = lax.dot_general(qm, k_ref[:, lo:hi], NT, preferred_element_type=f32) * score_scale
        s2 = lax.dot_general(qm, fk[:, lo:hi], NT, preferred_element_type=f32) * score_scale
        s1 = jnp.where(cache_live, s1, MESH_FLOOR)
        s2 = jnp.where(fresh_live, s2, MESH_FLOOR)
        peak = jnp.maximum(
            jnp.max(s1, axis=1, keepdims=True), jnp.max(s2, axis=1, keepdims=True)
        )
        e1 = jnp.where(cache_live, jnp.exp(s1 - peak), 0.0)
        e2 = jnp.where(fresh_live, jnp.exp(s2 - peak), 0.0)
        part = jnp.sum(e1, axis=1, keepdims=True) + jnp.sum(e2, axis=1, keepdims=True)
        o = jnp.dot(e1.astype(bf16), v_ref[:, lo:hi], preferred_element_type=f32) + jnp.dot(
            e2.astype(bf16), fv[:, lo:hi], preferred_element_type=f32
        )
        safe = jnp.maximum(part, 1e-30)
        lse = jnp.where(part > 0.0, peak + jnp.log(safe), MESH_FLOOR)
        os_[g, :, :rows_g, :] = (o / safe).astype(bf16).reshape(n, rows_g, HEAD_WIDTH)
        stat = jnp.sum(jnp.where(eye, lse.reshape(n, rows_g, 1), 0.0), axis=1, keepdims=True)
        high = stat.astype(bf16).astype(f32)
        mid = (stat - high).astype(bf16).astype(f32)
        low = stat - high - mid
        os_[g, :, rows_g:, :] = jnp.where(
            term == 0, high, jnp.where(term == 1, mid, jnp.where(term == 2, low, 0.0))
        ).astype(bf16)
        scatter(2 + g, lambda d: os_.at[g, d], lambda i: og.at[g, i])
        og[g, me] = os_[g, me]

    for g in range(groups):
        gathered(2 + g, lambda i: og.at[g, i])
        stat = jnp.sum(og[g, :, rows_g:, :].astype(f32), axis=1, keepdims=True)
        share = jnp.exp(stat - jnp.max(stat, axis=0, keepdims=True))
        share = share / jnp.sum(share, axis=0, keepdims=True)
        share = jnp.sum(jnp.where(eye, share, 0.0), axis=2, keepdims=True)
        part_o = og[g, :, :rows_g, :].astype(f32)
        av = jnp.sum(share * part_o, axis=0).astype(bf16)
        part = pl.ds(g * rows_g, rows_g)
        ats[g * rows_g : (g + 1) * rows_g, :] = av
        atg[me, g * rows_g : (g + 1) * rows_g, :] = av
        scatter(4 + g, lambda d: ats.at[part], lambda i: atg.at[i, part])
    op_copy.wait()
    proj = jnp.zeros((tokens, cols), f32)
    for g in range(groups):
        part = pl.ds(g * rows_g, rows_g)
        gathered(4 + g, lambda i: atg.at[i, part])
        af = atg[:, g * rows_g : (g + 1) * rows_g, :].astype(f32)
        attended = jnp.concatenate(
            [af[:, h * tok : (h + 1) * tok, :].reshape(tokens, HEAD_WIDTH) for h in range(ratio)],
            axis=1,
        ).astype(bf16)
        depth = ratio * HEAD_WIDTH
        proj += jnp.dot(
            attended, op_v[g * depth : (g + 1) * depth, :], preferred_element_type=f32
        )
    ps[...] = proj
    swap = partner(0, ps, pr)
    swap.start()
    gathered(6, lambda i: info_g.at[i])
    gathered(7, lambda i: rg.at[i])
    rf = rg[...].astype(f32)
    resid = jnp.concatenate(
        [rf[:, :tok, :].reshape(tokens, half), rf[:, tok:, :].reshape(tokens, half)], axis=1
    )
    slot_all = jnp.sum(info_g[:, 0:1, :], axis=0).astype(jnp.int32)
    lane_p = lax.broadcasted_iota(jnp.int32, (packed_rows, 128), 1)
    row_p = lax.broadcasted_iota(jnp.int32, (packed_rows, 128), 0)
    place = (lane_p >> 3) * SLOTS + slot_all - 1
    select = jnp.where((row_p == place) & (slot_all > 0), 1.0, 0.0)[:, :tokens].astype(bf16)
    swap.wait_recv()
    hidden = (resid + (proj + pr[...])).astype(bf16)
    hp = jnp.dot(select, hidden, preferred_element_type=f32)
    hv = jnp.concatenate([hp[:, :half], hp[:, half:]], axis=0).astype(bf16)
    hs[...] = hv
    hg[me] = hv
    scatter(8, lambda d: hs, lambda i: hg.at[i])
    hf = hidden.astype(f32)
    for j in range(n):
        block = hf[j * tok : (j + 1) * tok, :]
        xs[j] = jnp.concatenate([block[:, :half], block[:, half:]], axis=0).astype(bf16)
    scatter(9, lambda d: xs.at[d], lambda i: xg.at[i])
    xg[me] = xs[me]

    col_tile = piece
    acc[...] = jnp.zeros_like(acc)

    def gate_step(k, squares):
        j = lax.rem(me + k, n)

        @pl.when(k > 0)
        def _():
            arrived(8, lambda i: hg.at[i], j)

        hb = hg[j].astype(f32)
        x = jnp.concatenate([hb[:packed_rows], hb[packed_rows:]], axis=1)
        xb = (x * gain_ref[j]).astype(bf16)
        normed[j] = xb
        gate_copy(j).wait()

        w = w_v[pl.ds(pl.multiple_of(j * cols, cols), cols), :]
        acc[0] += jnp.dot(xb, w, preferred_element_type=f32)
        return squares + jnp.sum(x * x, axis=1, keepdims=True)

    squares = lax.fori_loop(0, n, gate_step, jnp.zeros((packed_rows, 1), f32))
    for i in range(1, 2 * PIECES):
        down_copy(i).start()

    each(lambda j: up_copy(j).wait())
    every = jnp.concatenate([normed[j] for j in range(n)], axis=1)
    up_tile = ff // 2

    def up_step(c, z):
        at = pl.ds(pl.multiple_of(c * up_tile, up_tile), up_tile)
        acc[1, :, at] = jnp.dot(every, w_v[width:, at], preferred_element_type=f32)
        return z

    lax.fori_loop(0, ff // up_tile, up_step, 0)
    factor = lax.rsqrt(squares / width + 1e-5)
    gate = acc[0] * factor
    up = acc[1] * factor
    act = (gate / (1.0 + jnp.exp(-gate)) * up).astype(bf16)

    for p in range(PIECES):
        down_copy(2 * p).wait()
        down_copy(2 * p + 1).wait()
        for c in range(piece // col_tile):
            at = slice(c * col_tile, (c + 1) * col_tile)
            first = wd_v[:, at] if p == 0 else w_v[(2 * p - 1) * wd_half : 2 * p * wd_half, at]
            second = w_v[2 * p * wd_half : (2 * p + 1) * wd_half, at]
            d = jnp.dot(act[:, :wd_half], first, preferred_element_type=f32)
            d += jnp.dot(act[:, wd_half:], second, preferred_element_type=f32)
            for t in range(col_tile // 128):
                spread[pl.ds(c * (col_tile // 128) + t, packed_rows, stride=tiles), :] = d[
                    :, t * 128 : (t + 1) * 128
                ]
        ys[p] = spread[...].astype(bf16).reshape(n, SLOTS * tiles, 128)
        yg[p, me] = ys[p, me]
        scatter(10 + p, lambda d: ys.at[p, d], lambda i: yg.at[p, i])

    swaps = []
    for p in range(PIECES):
        gathered(10 + p, lambda i: yg.at[p, i])
        total[p] = jnp.sum(yg[p].astype(f32), axis=0)
        for t in range(tiles):
            mixed = jnp.zeros((tok, 128), f32)
            for s in range(SLOTS):
                weight = jnp.where(slot1 == s + 1.0, gate_w, 0.0)
                mixed += weight * total[p, s * tiles + t : s * tiles + t + 1, :]
            ms[p, :, t * 128 : (t + 1) * 128] = mixed
        swaps.append(partner(1 + p, ms.at[p], mr.at[p]))
        swaps[-1].start()
    gathered(9, lambda i: xg.at[i])
    own = []
    for j in range(n):
        block = xg[j].astype(f32)
        own.append(jnp.concatenate([block[:tok], block[tok:]], axis=1))
    own = jnp.concatenate(own, axis=1)
    for p in range(PIECES):
        swaps[p].wait_recv()
        at = slice(p * piece, (p + 1) * piece)
        out_ref[:, at] = (own[:, at] + (ms[p] + mr[p])).astype(bf16)

    def sent(phase, src):
        each(lambda d: remote(phase, src(d), src(d), d, d).wait_send(), 1)

    for g in range(groups):
        part = pl.ds(g * rows_g, rows_g)
        sent(g, lambda d: qs.at[part])
        sent(2 + g, lambda d: os_.at[g, d])
        sent(4 + g, lambda d: ats.at[part])
    sent(6, lambda d: info_s)
    sent(7, lambda d: rs.at[d])
    sent(8, lambda d: hs)
    sent(9, lambda d: xs.at[d])
    for p in range(PIECES):
        sent(10 + p, lambda d: ys.at[p, d])
    swap.wait_send()
    for s in swaps:
        s.wait_send()


def one_kernel(
    queries, fresh_keys, fresh_values, prefix_key_cache, prefix_value_cache, prefix_len,
    residual, out_proj, norm_gain, routes, route_weight, w_gate, w_up, w_down,
):
    n = lax.axis_size("ctx")
    tok, width = residual.shape
    cols = width // n
    half = cols // 2
    head_rows = queries.shape[1] // HEAD_WIDTH * tok
    groups = prefix_key_cache.shape[1] // HEAD_WIDTH
    tokens = n * tok
    ff = w_gate.shape[2]
    piece = width // PIECES
    prow = n * SLOTS
    f32, bf16 = jnp.float32, jnp.bfloat16
    V = pltpu.VMEM
    vmem = pl.BlockSpec(memory_space=pltpu.VMEM)
    hbm = pl.BlockSpec(memory_space=pl.ANY)
    return pl.pallas_call(
        functools.partial(layer_kernel, n),
        out_shape=jax.ShapeDtypeStruct(residual.shape, bf16),
        in_specs=[pl.BlockSpec(memory_space=pltpu.SMEM)] + [vmem] * 9 + [hbm] * 4,
        out_specs=vmem,
        scratch_shapes=[
            V((2 * width, ff), bf16),
            V((ff // 2, piece), bf16),
            V(out_proj.shape, bf16),
            V((head_rows, HEAD_WIDTH), bf16),
            V((n, head_rows, HEAD_WIDTH), bf16),
            V((8, 128), f32),
            V((n, 8, 128), f32),
            V((n, 2 * tok, half), bf16),
            V((n, 2 * tok, half), bf16),
            V((groups, n, head_rows // groups + 16, HEAD_WIDTH), bf16),
            V((groups, n, head_rows // groups + 16, HEAD_WIDTH), bf16),
            V((head_rows, HEAD_WIDTH), bf16),
            V((n, head_rows, HEAD_WIDTH), bf16),
            V((tokens, cols), f32),
            V((tokens, cols), f32),
            V((2 * prow, half), bf16),
            V((n, 2 * prow, half), bf16),
            V((n, 2 * tok, half), bf16),
            V((n, 2 * tok, half), bf16),
            V((n, prow, cols), bf16),
            V((2, prow, ff), f32),
            V((prow * (piece // 128), 128), f32),
            V((PIECES, n, SLOTS * (piece // 128), 128), bf16),
            V((PIECES, n, SLOTS * (piece // 128), 128), bf16),
            V((PIECES, SLOTS * (piece // 128), 128), f32),
            V((PIECES, tok, piece), f32),
            V((PIECES, tok, piece), f32),
            pltpu.SemaphoreType.DMA((1 + 2 * n + 2 * PIECES,)),
            pltpu.SemaphoreType.DMA((10 + PIECES, n)),
            pltpu.SemaphoreType.DMA((10 + PIECES, n)),
            pltpu.SemaphoreType.DMA((1 + PIECES,)),
            pltpu.SemaphoreType.DMA((1 + PIECES,)),
        ],
        compiler_params=pltpu.CompilerParams(
            collective_id=0, has_side_effects=True, vmem_limit_bytes=63 * 2**20
        ),
        name="prefill_layer",
    )(
        prefix_len, queries, fresh_keys, fresh_values, prefix_key_cache, prefix_value_cache,
        residual, norm_gain.reshape(n, 1, cols), routes.T, route_weight.T, out_proj,
        w_gate.reshape(w_gate.shape[1:]), w_up.reshape(w_up.shape[1:]),
        w_down.reshape(w_down.shape[1:]),
    )


def layer(*args):
    queries, w_gate, residual = args[0], args[11], args[6]
    n = lax.axis_size("ctx")
    tokens = n * residual.shape[0]
    width, ff = w_gate.shape[1:]
    fits = tokens <= 128 and residual.shape[0] == 8 and width == PIECES * ff
    fits = fits and width % (n * 256) == 0 and lax.axis_size("exp") == 2
    return one_kernel(*args) if fits else on_device(*args)


def solution(mesh):
    return jax.shard_map(
        layer,
        mesh=mesh,
        in_specs=(
            P(("grp", "ctx"), "exp"),
            P(("grp", "ctx"), "exp"),
            P(("grp", "ctx"), "exp"),
            P(("grp", "ctx"), "exp"),
            P(("grp", "ctx"), "exp"),
            P("grp"),
            P(("grp", "ctx"), None),
            P("exp", "ctx"),
            P(),
            P(("grp", "ctx"), None),
            P(("grp", "ctx"), None),
            P("exp", None, "ctx"),
            P("exp", None, "ctx"),
            P("exp", "ctx", None),
        ),
        out_specs=P(("grp", "ctx"), None),
        check_vma=False,
    )
```

```python
import functools
import math

import jax
import jax.numpy as jnp
from jax import lax
from jax.experimental import pallas as pl
from jax.experimental.pallas import tpu as pltpu
from jax.sharding import PartitionSpec as P

HEAD_WIDTH = 128
SLOTS = 3


masked_floor = -1e30


def on_device(
    queries,
    fresh_keys,
    fresh_values,
    prefix_key_cache,
    prefix_value_cache,
    prefix_len,
    residual,
    out_proj,
    norm_gain,
    routes,
    route_weight,
    w_gate,
    w_up,
    w_down,
):
    tok_dev = queries.shape[0]
    cache_dev = prefix_key_cache.shape[0]
    n_ctx = lax.axis_size("ctx")
    tokens = tok_dev * n_ctx
    heads_dev = queries.shape[1] // HEAD_WIDTH
    groups = prefix_key_cache.shape[1] // HEAD_WIDTH
    ratio_q = heads_dev // groups
    key_count = cache_dev + tok_dev
    score_scale = 1.0 / math.sqrt(HEAD_WIDTH)
    ctx_rank = lax.axis_index("ctx")
    key_matrix = jnp.concatenate([prefix_key_cache, fresh_keys], axis=0).reshape(
        key_count, groups, HEAD_WIDTH
    )
    value_matrix = jnp.concatenate([prefix_value_cache, fresh_values], axis=0).reshape(
        key_count, groups, HEAD_WIDTH
    )
    cache_live = ctx_rank * cache_dev + jnp.arange(cache_dev, dtype=jnp.int32) < prefix_len[0]
    span_index = ctx_rank * tok_dev + jnp.arange(tok_dev, dtype=jnp.int32)
    all_queries = lax.all_gather(queries, "ctx", axis=0, tiled=True)
    block_of_rows = min(512, tokens)
    block_count = tokens // block_of_rows

    def block_setup(block_index):
        row_start = block_index * block_of_rows
        query_matrix = all_queries.reshape(block_of_rows, groups, ratio_q, HEAD_WIDTH)
        scores = (
            jnp.einsum(
                "bgrd,kgd->bgrk", query_matrix, key_matrix, preferred_element_type=jnp.float32
            )
            * score_scale
        )
        query_index = row_start + jnp.arange(block_of_rows, dtype=jnp.int32)
        visible = jnp.concatenate(
            [
                jnp.broadcast_to(cache_live[None, :], (block_of_rows, cache_dev)),
                span_index[None, :] <= query_index[:, None],
            ],
            axis=1,
        )[:, None, None, :]
        return (scores, visible)

    def block_peaks(block_index):
        scores, visible = block_setup(block_index)
        return jnp.max(jnp.where(visible, scores, masked_floor), axis=-1).reshape(
            block_of_rows, heads_dev
        )

    local_peak = lax.map(block_peaks, jnp.arange(block_count, dtype=jnp.int32))
    global_peak = lax.pmax(local_peak, "ctx")

    def block_partials(operands):
        block_index, peak_rows = operands
        scores, visible = block_setup(block_index)
        peak_full = peak_rows.reshape(block_of_rows, groups, ratio_q)
        exponent = jnp.where(visible, jnp.exp(scores - peak_full[..., None]), 0.0)
        row_total = jnp.sum(exponent, axis=-1)
        weighted = jnp.einsum(
            "bgrk,kgd->bgrd",
            exponent.astype(jnp.bfloat16),
            value_matrix,
            preferred_element_type=jnp.float32,
        )
        return (
            weighted.reshape(block_of_rows, heads_dev, HEAD_WIDTH),
            row_total.reshape(block_of_rows, heads_dev),
        )

    weighted, row_total = lax.map(
        block_partials, (jnp.arange(block_count, dtype=jnp.int32), global_peak)
    )
    weighted = weighted.reshape(tokens, heads_dev, HEAD_WIDTH)
    row_total = row_total.reshape(tokens, heads_dev)
    got_weighted, got_total = (
        lax.all_to_all(
            weighted.reshape(n_ctx, tok_dev, heads_dev, HEAD_WIDTH),
            "ctx",
            split_axis=0,
            concat_axis=0,
            tiled=True,
        ),
        lax.all_to_all(
            row_total.reshape(n_ctx, tok_dev, heads_dev),
            "ctx",
            split_axis=0,
            concat_axis=0,
            tiled=True,
        ),
    )
    numer = jnp.sum(got_weighted, axis=0)
    denom = jnp.sum(got_total, axis=0)
    attended = (
        (numer / denom[..., None]).reshape(tok_dev, heads_dev * HEAD_WIDTH).astype(jnp.bfloat16)
    )
    projected = jnp.dot(
        lax.all_gather(attended, "ctx", axis=0, tiled=True),
        out_proj,
        preferred_element_type=jnp.float32,
    )
    col_dev = projected.shape[1]
    token_cols = lax.all_to_all(
        projected.reshape(n_ctx, tok_dev, col_dev), "ctx", split_axis=0, concat_axis=2, tiled=True
    )
    attn_rows = lax.psum(token_cols.reshape(tok_dev, n_ctx * col_dev), "exp")
    hidden = (residual.astype(jnp.float32) + attn_rows).astype(jnp.bfloat16)
    hidden_f = hidden.astype(jnp.float32)
    normed = (
        hidden_f
        * lax.rsqrt(jnp.mean(hidden_f * hidden_f, axis=-1, keepdims=True) + 1e-05)
        * norm_gain
    ).astype(jnp.bfloat16)
    expert = lax.axis_index("exp")
    route_hits = routes == expert
    chosen = jnp.any(route_hits, axis=-1)
    gate_w = jnp.sum(jnp.where(route_hits, route_weight, 0.0), axis=-1)
    slot_rank = jnp.cumsum(chosen.astype(jnp.int32)) - 1
    slot_ids = jnp.arange(SLOTS, dtype=jnp.int32)
    onehot = ((slot_rank[None, :] == slot_ids[:, None]) & chosen[None, :]).astype(jnp.bfloat16)
    packed = jnp.dot(onehot, normed, preferred_element_type=jnp.float32).astype(jnp.bfloat16)
    gate_mat = w_gate[0]
    up_mat = w_up[0]
    down_mat = w_down[0]
    shard_rows = lax.all_gather(packed, "ctx", axis=0, tiled=True)
    gate_proj = jnp.dot(shard_rows, gate_mat, preferred_element_type=jnp.float32)
    up_proj = jnp.dot(shard_rows, up_mat, preferred_element_type=jnp.float32)
    activation = (jax.nn.silu(gate_proj) * up_proj).astype(jnp.bfloat16)
    own_sums = lax.psum_scatter(
        jnp.dot(activation, down_mat, preferred_element_type=jnp.float32),
        "ctx",
        scatter_dimension=0,
        tiled=True,
    )
    unpacked = jnp.dot(onehot.astype(jnp.float32).T, own_sums, precision=lax.Precision.HIGHEST)
    mixed = lax.psum(unpacked * gate_w[:, None], "exp")
    return (hidden_f + mixed).astype(jnp.bfloat16)


MESH_FLOOR = -1e30
NT = (((1,), (1,)), ((), ()))
PIECES = 3


def layer_kernel(
    n, plen_ref, q_ref, fk_ref, fv_ref, k_ref, v_ref, res_ref, gain_ref, routes_ref, rw_ref,
    op_hbm, wg_hbm, wu_hbm, wd_hbm, out_ref,
    w_v, wd_v, op_v, qs, qg, info_s, info_g, rs, rg, os_, og, ats, atg, ps, pr,
    hs, hg, xs, xg, normed, acc, spread, ys, yg, total, ms, mr,
    lsem, send, recv, psend, precv,
):
    f32, bf16 = jnp.float32, jnp.bfloat16
    me = lax.axis_index("ctx")
    expert = lax.axis_index("exp")
    tok, width = res_ref.shape
    cols = width // n
    half = cols // 2
    head_count = q_ref.shape[1] // HEAD_WIDTH
    groups = k_ref.shape[1] // HEAD_WIDTH
    ratio = head_count // groups
    rows_g = ratio * tok
    cache = k_ref.shape[0]
    tokens = n * tok
    packed_rows = n * SLOTS
    ff = wg_hbm.shape[1]
    piece = width // PIECES
    tiles = piece // 128
    wd_half = ff // 2

    op_copy = pltpu.make_async_copy(op_hbm, op_v, lsem.at[0])
    op_copy.start()

    def gate_copy(j):
        return pltpu.make_async_copy(
            wg_hbm.at[pl.ds(j * cols, cols), :], w_v.at[pl.ds(j * cols, cols), :], lsem.at[1 + j]
        )

    def up_copy(j):
        return pltpu.make_async_copy(
            wu_hbm.at[pl.ds(j * cols, cols), :],
            w_v.at[pl.ds(width + j * cols, cols), :],
            lsem.at[1 + n + j],
        )

    def down_copy(i):
        p, h = i // 2, i % 2
        src = wd_hbm.at[pl.ds(h * wd_half, wd_half), pl.ds(p * piece, piece)]
        dst = wd_v if i == 0 else w_v.at[pl.ds((i - 1) * wd_half, wd_half), :]
        return pltpu.make_async_copy(src, dst, lsem.at[1 + 2 * n + i])

    def each(body, first=0):
        def step(k, c):
            body(lax.rem(me + k, n))
            return c

        lax.fori_loop(first, n, step, 0)

    each(lambda j: gate_copy(j).start())
    each(lambda j: up_copy(j).start())
    down_copy(0).start()

    barrier = pltpu.get_barrier_semaphore()

    def greet(d):
        pl.semaphore_signal(
            barrier, inc=1, device_id={"ctx": d}, device_id_type=pl.DeviceIdType.MESH
        )

    each(greet, 1)
    pl.semaphore_signal(
        barrier, inc=1, device_id={"exp": 1 - expert}, device_id_type=pl.DeviceIdType.MESH
    )

    def remote(phase, src, dst, d, slot):
        return pltpu.make_async_remote_copy(
            src_ref=src, dst_ref=dst, send_sem=send.at[phase, d], recv_sem=recv.at[phase, slot],
            device_id={"ctx": d}, device_id_type=pl.DeviceIdType.MESH,
        )

    def scatter(phase, src_of, dst_of):
        each(lambda d: remote(phase, src_of(d), dst_of(me), d, me).start(), 1)

    def arrived(phase, dst_of, i):
        remote(phase, dst_of(i), dst_of(i), i, i).wait_recv()

    def gathered(phase, dst_of):
        each(lambda i: arrived(phase, dst_of, i), 1)

    def partner(i, src, dst):
        return pltpu.make_async_remote_copy(
            src_ref=src, dst_ref=dst, send_sem=psend.at[i], recv_sem=precv.at[i],
            device_id={"exp": 1 - expert}, device_id_type=pl.DeviceIdType.MESH,
        )

    q = q_ref[...].astype(f32)
    qv = jnp.concatenate(
        [q[:, h * HEAD_WIDTH : (h + 1) * HEAD_WIDTH] for h in range(head_count)], axis=0
    ).astype(bf16)
    qs[...] = qv
    qg[me] = qv

    hit = (routes_ref[...] == expert).astype(f32)
    chosen_row = jnp.max(hit, axis=0, keepdims=True)
    weight_row = jnp.sum(hit * rw_ref[...], axis=0, keepdims=True)
    lane_t = lax.broadcasted_iota(jnp.int32, (tok, tok), 1)
    sub_t = lax.broadcasted_iota(jnp.int32, (tok, tok), 0)

    def column(keep, row):
        return jnp.sum(jnp.where(keep, row, 0.0), axis=1, keepdims=True)

    chosen = column(lane_t == sub_t, chosen_row)
    gate_w = column(lane_t == sub_t, weight_row)
    rank = column(lane_t < sub_t, chosen_row)
    slot1 = jnp.where(chosen > 0.0, rank + 1.0, 0.0)
    lane = lax.broadcasted_iota(jnp.int32, (tok, 128), 1)
    sub = lax.broadcasted_iota(jnp.int32, (tok, 128), 0)
    slot_row = jnp.sum(jnp.where(lane == sub + me * tok, slot1, 0.0), axis=0, keepdims=True)
    info = jnp.broadcast_to(slot_row, (8, 128))
    info_s[...] = info
    info_g[me] = info

    res = res_ref[...].astype(f32)
    for j in range(n):
        block = res[:, j * cols : (j + 1) * cols]
        rs[j] = jnp.concatenate([block[:, :half], block[:, half:]], axis=0).astype(bf16)

    pl.semaphore_wait(barrier, n)
    for g in range(groups):
        part = pl.ds(g * rows_g, rows_g)
        scatter(g, lambda d: qs.at[part], lambda i: qg.at[i, part])
    scatter(6, lambda d: info_s, lambda i: info_g.at[i])
    scatter(7, lambda d: rs.at[d], lambda i: rg.at[i])
    rg[me] = rs[me]

    prefix = plen_ref[0]
    pad = jnp.zeros((128 - tok, groups * HEAD_WIDTH), f32)
    fk = jnp.concatenate([fk_ref[...].astype(f32), pad], axis=0).astype(bf16)
    fv = jnp.concatenate([fv_ref[...].astype(f32), pad], axis=0).astype(bf16)
    rows = n * rows_g
    cache_live = me * cache + lax.broadcasted_iota(jnp.int32, (1, cache), 1) < prefix
    row_token = lax.broadcasted_iota(jnp.int32, (n, rows_g, 128), 0) * tok + (
        lax.broadcasted_iota(jnp.int32, (n, rows_g, 128), 1) & (tok - 1)
    )
    key_lane = lax.broadcasted_iota(jnp.int32, (n, rows_g, 128), 2)
    fresh_live = jnp.where(
        (key_lane < tok) & (me * tok + key_lane <= row_token), 1, 0
    ).reshape(rows, 128) > 0
    eye = lax.broadcasted_iota(jnp.int32, (1, rows_g, 128), 1) == lax.broadcasted_iota(
        jnp.int32, (1, rows_g, 128), 2
    )
    score_scale = 1.0 / math.sqrt(HEAD_WIDTH)
    term = lax.broadcasted_iota(jnp.int32, (n, 16, 128), 1)
    for g in range(groups):
        lo, hi = g * HEAD_WIDTH, (g + 1) * HEAD_WIDTH
        part = pl.ds(g * rows_g, rows_g)
        gathered(g, lambda i: qg.at[i, part])
        qm = qg[:, g * rows_g : (g + 1) * rows_g, :].reshape(rows, HEAD_WIDTH)
        s1 = lax.dot_general(qm, k_ref[:, lo:hi], NT, preferred_element_type=f32) * score_scale
        s2 = lax.dot_general(qm, fk[:, lo:hi], NT, preferred_element_type=f32) * score_scale
        s1 = jnp.where(cache_live, s1, MESH_FLOOR)
        s2 = jnp.where(fresh_live, s2, MESH_FLOOR)
        peak = jnp.maximum(
            jnp.max(s1, axis=1, keepdims=True), jnp.max(s2, axis=1, keepdims=True)
        )
        e1 = jnp.where(cache_live, jnp.exp(s1 - peak), 0.0)
        e2 = jnp.where(fresh_live, jnp.exp(s2 - peak), 0.0)
        part = jnp.sum(e1, axis=1, keepdims=True) + jnp.sum(e2, axis=1, keepdims=True)
        o = jnp.dot(e1.astype(bf16), v_ref[:, lo:hi], preferred_element_type=f32) + jnp.dot(
            e2.astype(bf16), fv[:, lo:hi], preferred_element_type=f32
        )
        safe = jnp.maximum(part, 1e-30)
        lse = jnp.where(part > 0.0, peak + jnp.log(safe), MESH_FLOOR)
        os_[g, :, :rows_g, :] = (o / safe).astype(bf16).reshape(n, rows_g, HEAD_WIDTH)
        stat = jnp.sum(jnp.where(eye, lse.reshape(n, rows_g, 1), 0.0), axis=1, keepdims=True)
        high = stat.astype(bf16).astype(f32)
        mid = (stat - high).astype(bf16).astype(f32)
        low = stat - high - mid
        os_[g, :, rows_g:, :] = jnp.where(
            term == 0, high, jnp.where(term == 1, mid, jnp.where(term == 2, low, 0.0))
        ).astype(bf16)
        scatter(2 + g, lambda d: os_.at[g, d], lambda i: og.at[g, i])
        og[g, me] = os_[g, me]

    for g in range(groups):
        gathered(2 + g, lambda i: og.at[g, i])
        stat = jnp.sum(og[g, :, rows_g:, :].astype(f32), axis=1, keepdims=True)
        share = jnp.exp(stat - jnp.max(stat, axis=0, keepdims=True))
        share = share / jnp.sum(share, axis=0, keepdims=True)
        share = jnp.sum(jnp.where(eye, share, 0.0), axis=2, keepdims=True)
        part_o = og[g, :, :rows_g, :].astype(f32)
        av = jnp.sum(share * part_o, axis=0).astype(bf16)
        part = pl.ds(g * rows_g, rows_g)
        ats[g * rows_g : (g + 1) * rows_g, :] = av
        atg[me, g * rows_g : (g + 1) * rows_g, :] = av
        scatter(4 + g, lambda d: ats.at[part], lambda i: atg.at[i, part])
    op_copy.wait()
    proj = jnp.zeros((tokens, cols), f32)
    for g in range(groups):
        part = pl.ds(g * rows_g, rows_g)
        gathered(4 + g, lambda i: atg.at[i, part])
        af = atg[:, g * rows_g : (g + 1) * rows_g, :].astype(f32)
        attended = jnp.concatenate(
            [af[:, h * tok : (h + 1) * tok, :].reshape(tokens, HEAD_WIDTH) for h in range(ratio)],
            axis=1,
        ).astype(bf16)
        depth = ratio * HEAD_WIDTH
        proj += jnp.dot(
            attended, op_v[g * depth : (g + 1) * depth, :], preferred_element_type=f32
        )
    ps[...] = proj
    swap = partner(0, ps, pr)
    swap.start()
    gathered(6, lambda i: info_g.at[i])
    gathered(7, lambda i: rg.at[i])
    rf = rg[...].astype(f32)
    resid = jnp.concatenate(
        [rf[:, :tok, :].reshape(tokens, half), rf[:, tok:, :].reshape(tokens, half)], axis=1
    )
    slot_all = jnp.sum(info_g[:, 0:1, :], axis=0).astype(jnp.int32)
    lane_p = lax.broadcasted_iota(jnp.int32, (packed_rows, 128), 1)
    row_p = lax.broadcasted_iota(jnp.int32, (packed_rows, 128), 0)
    place = (lane_p >> 3) * SLOTS + slot_all - 1
    select = jnp.where((row_p == place) & (slot_all > 0), 1.0, 0.0)[:, :tokens].astype(bf16)
    swap.wait_recv()
    hidden = (resid + (proj + pr[...])).astype(bf16)
    hp = jnp.dot(select, hidden, preferred_element_type=f32)
    hv = jnp.concatenate([hp[:, :half], hp[:, half:]], axis=0).astype(bf16)
    hs[...] = hv
    hg[me] = hv
    scatter(8, lambda d: hs, lambda i: hg.at[i])
    hf = hidden.astype(f32)
    for j in range(n):
        block = hf[j * tok : (j + 1) * tok, :]
        xs[j] = jnp.concatenate([block[:, :half], block[:, half:]], axis=0).astype(bf16)
    scatter(9, lambda d: xs.at[d], lambda i: xg.at[i])
    xg[me] = xs[me]

    col_tile = piece
    acc[...] = jnp.zeros_like(acc)

    def gate_step(k, squares):
        j = lax.rem(me + n - k, n)

        @pl.when(k > 0)
        def _():
            arrived(8, lambda i: hg.at[i], j)

        hb = hg[j].astype(f32)
        x = jnp.concatenate([hb[:packed_rows], hb[packed_rows:]], axis=1)
        xb = (x * gain_ref[j]).astype(bf16)
        normed[j] = xb
        gate_copy(j).wait()

        w = w_v[pl.ds(pl.multiple_of(j * cols, cols), cols), :]
        acc[0] += jnp.dot(xb, w, preferred_element_type=f32)
        return squares + jnp.sum(x * x, axis=1, keepdims=True)

    squares = lax.fori_loop(0, n, gate_step, jnp.zeros((packed_rows, 1), f32))
    for i in range(1, 2 * PIECES):
        down_copy(i).start()

    each(lambda j: up_copy(j).wait())
    every = jnp.concatenate([normed[j] for j in range(n)], axis=1)
    up_tile = ff // 2

    def up_step(c, z):
        at = pl.ds(pl.multiple_of(c * up_tile, up_tile), up_tile)
        acc[1, :, at] = jnp.dot(every, w_v[width:, at], preferred_element_type=f32)
        return z

    lax.fori_loop(0, ff // up_tile, up_step, 0)
    factor = lax.rsqrt(squares / width + 1e-5)
    gate = acc[0] * factor
    up = acc[1] * factor
    act = (gate / (1.0 + jnp.exp(-gate)) * up).astype(bf16)

    for p in range(PIECES):
        down_copy(2 * p).wait()
        down_copy(2 * p + 1).wait()
        for c in range(piece // col_tile):
            at = slice(c * col_tile, (c + 1) * col_tile)
            first = wd_v[:, at] if p == 0 else w_v[(2 * p - 1) * wd_half : 2 * p * wd_half, at]
            second = w_v[2 * p * wd_half : (2 * p + 1) * wd_half, at]
            d = jnp.dot(act[:, :wd_half], first, preferred_element_type=f32)
            d += jnp.dot(act[:, wd_half:], second, preferred_element_type=f32)
            for t in range(col_tile // 128):
                spread[pl.ds(c * (col_tile // 128) + t, packed_rows, stride=tiles), :] = d[
                    :, t * 128 : (t + 1) * 128
                ]
        ys[p] = spread[...].astype(bf16).reshape(n, SLOTS * tiles, 128)
        yg[p, me] = ys[p, me]
        scatter(10 + p, lambda d: ys.at[p, d], lambda i: yg.at[p, i])

    swaps = []
    for p in range(PIECES):
        gathered(10 + p, lambda i: yg.at[p, i])
        total[p] = jnp.sum(yg[p].astype(f32), axis=0)
        for t in range(tiles):
            mixed = jnp.zeros((tok, 128), f32)
            for s in range(SLOTS):
                weight = jnp.where(slot1 == s + 1.0, gate_w, 0.0)
                mixed += weight * total[p, s * tiles + t : s * tiles + t + 1, :]
            ms[p, :, t * 128 : (t + 1) * 128] = mixed
        swaps.append(partner(1 + p, ms.at[p], mr.at[p]))
        swaps[-1].start()
    gathered(9, lambda i: xg.at[i])
    own = []
    for j in range(n):
        block = xg[j].astype(f32)
        own.append(jnp.concatenate([block[:tok], block[tok:]], axis=1))
    own = jnp.concatenate(own, axis=1)
    for p in range(PIECES):
        swaps[p].wait_recv()
        at = slice(p * piece, (p + 1) * piece)
        out_ref[:, at] = (own[:, at] + (ms[p] + mr[p])).astype(bf16)

    def sent(phase, src):
        each(lambda d: remote(phase, src(d), src(d), d, d).wait_send(), 1)

    for g in range(groups):
        part = pl.ds(g * rows_g, rows_g)
        sent(g, lambda d: qs.at[part])
        sent(2 + g, lambda d: os_.at[g, d])
        sent(4 + g, lambda d: ats.at[part])
    sent(6, lambda d: info_s)
    sent(7, lambda d: rs.at[d])
    sent(8, lambda d: hs)
    sent(9, lambda d: xs.at[d])
    for p in range(PIECES):
        sent(10 + p, lambda d: ys.at[p, d])
    swap.wait_send()
    for s in swaps:
        s.wait_send()


def one_kernel(
    queries, fresh_keys, fresh_values, prefix_key_cache, prefix_value_cache, prefix_len,
    residual, out_proj, norm_gain, routes, route_weight, w_gate, w_up, w_down,
):
    n = lax.axis_size("ctx")
    tok, width = residual.shape
    cols = width // n
    half = cols // 2
    head_rows = queries.shape[1] // HEAD_WIDTH * tok
    groups = prefix_key_cache.shape[1] // HEAD_WIDTH
    tokens = n * tok
    ff = w_gate.shape[2]
    piece = width // PIECES
    prow = n * SLOTS
    f32, bf16 = jnp.float32, jnp.bfloat16
    V = pltpu.VMEM
    vmem = pl.BlockSpec(memory_space=pltpu.VMEM)
    hbm = pl.BlockSpec(memory_space=pl.ANY)
    return pl.pallas_call(
        functools.partial(layer_kernel, n),
        out_shape=jax.ShapeDtypeStruct(residual.shape, bf16),
        in_specs=[pl.BlockSpec(memory_space=pltpu.SMEM)] + [vmem] * 9 + [hbm] * 4,
        out_specs=vmem,
        scratch_shapes=[
            V((2 * width, ff), bf16),
            V((ff // 2, piece), bf16),
            V(out_proj.shape, bf16),
            V((head_rows, HEAD_WIDTH), bf16),
            V((n, head_rows, HEAD_WIDTH), bf16),
            V((8, 128), f32),
            V((n, 8, 128), f32),
            V((n, 2 * tok, half), bf16),
            V((n, 2 * tok, half), bf16),
            V((groups, n, head_rows // groups + 16, HEAD_WIDTH), bf16),
            V((groups, n, head_rows // groups + 16, HEAD_WIDTH), bf16),
            V((head_rows, HEAD_WIDTH), bf16),
            V((n, head_rows, HEAD_WIDTH), bf16),
            V((tokens, cols), f32),
            V((tokens, cols), f32),
            V((2 * prow, half), bf16),
            V((n, 2 * prow, half), bf16),
            V((n, 2 * tok, half), bf16),
            V((n, 2 * tok, half), bf16),
            V((n, prow, cols), bf16),
            V((2, prow, ff), f32),
            V((prow * (piece // 128), 128), f32),
            V((PIECES, n, SLOTS * (piece // 128), 128), bf16),
            V((PIECES, n, SLOTS * (piece // 128), 128), bf16),
            V((PIECES, SLOTS * (piece // 128), 128), f32),
            V((PIECES, tok, piece), f32),
            V((PIECES, tok, piece), f32),
            pltpu.SemaphoreType.DMA((1 + 2 * n + 2 * PIECES,)),
            pltpu.SemaphoreType.DMA((10 + PIECES, n)),
            pltpu.SemaphoreType.DMA((10 + PIECES, n)),
            pltpu.SemaphoreType.DMA((1 + PIECES,)),
            pltpu.SemaphoreType.DMA((1 + PIECES,)),
        ],
        compiler_params=pltpu.CompilerParams(
            collective_id=0, has_side_effects=True, vmem_limit_bytes=63 * 2**20
        ),
        name="prefill_layer",
    )(
        prefix_len, queries, fresh_keys, fresh_values, prefix_key_cache, prefix_value_cache,
        residual, norm_gain.reshape(n, 1, cols), routes.T, route_weight.T, out_proj,
        w_gate.reshape(w_gate.shape[1:]), w_up.reshape(w_up.shape[1:]),
        w_down.reshape(w_down.shape[1:]),
    )


def layer(*args):
    queries, w_gate, residual = args[0], args[11], args[6]
    n = lax.axis_size("ctx")
    tokens = n * residual.shape[0]
    width, ff = w_gate.shape[1:]
    fits = tokens <= 128 and residual.shape[0] == 8 and width == PIECES * ff
    fits = fits and width % (n * 256) == 0 and lax.axis_size("exp") == 2
    return one_kernel(*args) if fits else on_device(*args)


def solution(mesh):
    return jax.shard_map(
        layer,
        mesh=mesh,
        in_specs=(
            P(("grp", "ctx"), "exp"),
            P(("grp", "ctx"), "exp"),
            P(("grp", "ctx"), "exp"),
            P(("grp", "ctx"), "exp"),
            P(("grp", "ctx"), "exp"),
            P("grp"),
            P(("grp", "ctx"), None),
            P("exp", "ctx"),
            P(),
            P(("grp", "ctx"), None),
            P(("grp", "ctx"), None),
            P("exp", None, "ctx"),
            P("exp", None, "ctx"),
            P("exp", "ctx", None),
        ),
        out_specs=P(("grp", "ctx"), None),
        check_vma=False,
    )
```
